32 devices in a mesh: lon: 8 (over z, y), ch: 4 (over x, core).
Axes of the slice: x: 2, y: 2, z: 4, core: 2. Of those that a mesh axis runs over, the one named last changes fastest.
Arguments:
- ocean_state: bfloat16 [400, 64, 1024], P('ch', None, 'lon'), may hold values from -6 to 6
- sea_mask: int32 [64, 1024], P(None, 'lon'), may hold values 0 or 1
- kernel: float32 [400, 49], P('ch'), may hold values from -0.875 to 0.875
- conv_bias: float32 [400], P('ch'), may hold values from -3 to 3
- norm_gain: float32 [400], replicated, may hold values from 0.1 to 1.9
- norm_bias: float32 [400], replicated, may hold values from -2 to 2
- weight_in: bfloat16 [400, 1600], replicated, may hold values from -0.3125 to 0.3125
- bias_in: float32 [1600], replicated, may hold values from -3 to 3
- weight_out: bfloat16 [1600, 400], replicated, may hold values from -0.15625 to 0.15625
- bias_out: float32 [400], replicated, may hold values from -3 to 3
- layer_scale: float32 [400], P('ch'), may hold values from 0.5 to 2
- cotangent: bfloat16 [400, 64, 1024], P('ch', None, 'lon'), may hold values from -6 to 6
Outputs:
- updated: bfloat16 [400, 64, 1024], P('ch', None, 'lon')
- grad_state: bfloat16 [400, 64, 1024], P('ch', None, 'lon')
- grad_weight_in: float32 [400, 1600], replicated
- grad_weight_out: float32 [1600, 400], replicated
The draws below stay inside these ranges and needn't reach their ends.
Inputs may be any that keep to these rules, and one draw needn't show every extreme that they name: `sea_mask`: 1 marks an ocean cell, 0 a land cell.
All inputs are finite; a program needn't handle non-finite values. No bound on the sum of `sea_mask` on one device may be relied on, other than what follows from the above.
Results may differ from the reference program's by a relative error of at most 0.0077.
Values may be sent and summed in bfloat16 or wider, within the bound.
A program may use at most 192 MiB of HBM per device.

```python
import math
import jax
import jax.numpy as jnp
from jax import lax

C = 400
HID = 1600
KW = 7
ROWS = 64
LON = 1024


def plant(drawn, own_key, low, largest):
    longest = drawn.shape.index(max(drawn.shape))
    spots = []
    for shift in (0, 1):
        where = [jax.random.randint(jax.random.fold_in(own_key, axis), (), 0, length) for axis, length in enumerate(drawn.shape)]
        where[longest] = (where[longest] + shift) % drawn.shape[longest]
        spots.append(tuple(where))
    return drawn.at[spots[0]].set(low).at[spots[1]].set(largest)


def level_of(stream_key, dims, shards, low, largest):
    gain, own = 1.0, jax.random.fold_in(stream_key, 6)
    for position, shards_of in shards:
        heights = jnp.exp(jax.random.uniform(jax.random.fold_in(own, position), (shards_of,), jnp.float32, low / len(shards), largest / len(shards)))
        gain = gain * jnp.repeat(heights, dims[position] // shards_of).reshape([-1 if axis == position else 1 for axis in range(len(dims))])
    return gain


def gaussian(own_key, shape, deviation, bound, pieces=(), kind=jnp.bfloat16):
    values = jax.random.normal(own_key, shape, jnp.float32) * deviation
    if len(pieces) > 0:
        values = level_of(own_key, shape, pieces, -0.22, 0.18) * values
    return jnp.clip(values, min=-bound, max=bound).astype(kind)


def setup_inputs(seed: int = 0) -> dict:
    streams_of = jax.random.split(jax.random.key(seed), 13)
    return {
        "ocean_state": gaussian(streams_of[0], (C, ROWS, LON), 1.0, 6.0, ((0, 4), (2, 8))),
        "sea_mask": plant((jax.random.randint(streams_of[1], (ROWS, LON), 0, 4) < 3).astype(jnp.int32), jax.random.fold_in(streams_of[1], 1), 0, 1),
        "kernel": gaussian(streams_of[2], (C, KW * KW), (KW * KW) ** -0.5, 0.875, ((0, 4),), jnp.float32),
        "conv_bias": gaussian(streams_of[3], (C,), 0.5, 3.0, ((0, 4),), jnp.float32),
        "norm_gain": jnp.clip(1.0 + 0.18 * jax.random.normal(streams_of[4], (C,), jnp.float32), 0.1, 1.9),
        "norm_bias": gaussian(streams_of[5], (C,), 0.3, 2.0, (), jnp.float32),
        "weight_in": gaussian(streams_of[6], (C, HID), C ** -0.5, 0.3125),
        "bias_in": gaussian(streams_of[7], (HID,), 0.5, 3.0, (), jnp.float32),
        "weight_out": gaussian(streams_of[8], (HID, C), HID ** -0.5, 0.15625),
        "bias_out": gaussian(streams_of[9], (C,), 0.5, 3.0, (), jnp.float32),
        "layer_scale": jnp.clip(jnp.exp(math.log(2.0) - 1.3862944 * jax.random.uniform(streams_of[10], (C,), jnp.float32) ** level_of(streams_of[10], (C,), ((0, 4),), -0.2, 0.2)), 0.5, 2.0),
        "cotangent": gaussian(streams_of[11], (C, ROWS, LON), 1.0, 6.0, ((0, 4), (2, 8))),
    }


root_coef = math.sqrt(2.0 / math.pi)
cubic_coef = 0.044715
norm_eps = 1e-06

def gelu_parts(pre_act):
    inner_arg = root_coef * (pre_act + cubic_coef * pre_act * pre_act * pre_act)
    tangent = jnp.tanh(inner_arg)
    gelu_value = 0.5 * pre_act * (1.0 + tangent)
    gelu_slope = 0.5 * (1.0 + tangent) + 0.5 * pre_act * (1.0 - tangent * tangent) * root_coef * (1.0 + 3.0 * cubic_coef * pre_act * pre_act)
    return (gelu_value, gelu_slope)

def depth_taps(padded, kernel, row_count, lon_cells):
    tap_total = jnp.zeros((padded.shape[0], row_count, lon_cells), jnp.float32)
    for row_off in range(KW):
        for col_off in range(KW):
            tap_total = tap_total + kernel[:, row_off * KW + col_off][:, None, None] * padded[:, row_off:row_off + row_count, col_off:col_off + lon_cells]
    return tap_total

def depth_back(padded_grad, kernel, row_count, lon_cells):
    span = KW - 1
    tap_total = jnp.zeros((padded_grad.shape[0], row_count, lon_cells), jnp.float32)
    for row_off in range(KW):
        for col_off in range(KW):
            tap_total = tap_total + kernel[:, row_off * KW + col_off][:, None, None] * padded_grad[:, span - row_off:span - row_off + row_count, span - col_off:span - col_off + lon_cells]
    return tap_total

def block_math(conv_cells, grad_cells, norm_gain, norm_bias, weight_in, bias_in, weight_out, bias_out):
    full_width = conv_cells.shape[0]
    values = conv_cells.astype(jnp.float32)
    mean_val = lax.optimization_barrier(jnp.sum(values, axis=0)) / full_width
    square = lax.optimization_barrier(jnp.sum(values * values, axis=0)) / full_width
    inv_std = lax.rsqrt(square - mean_val * mean_val + norm_eps)
    centred = (values - mean_val) * inv_std
    normed = (centred * norm_gain[:, None] + norm_bias[:, None]).astype(jnp.bfloat16)
    pre_act = jnp.dot(weight_in.T, normed, preferred_element_type=jnp.float32) + bias_in[:, None]
    gelu_value, gelu_slope = gelu_parts(pre_act)
    activation = gelu_value.astype(jnp.bfloat16)
    branch = (jnp.dot(weight_out.T, activation, preferred_element_type=jnp.float32) + bias_out[:, None]).astype(jnp.bfloat16)
    grad_act = jnp.dot(weight_out, grad_cells, preferred_element_type=jnp.float32)
    grad_pre = (grad_act * gelu_slope).astype(jnp.bfloat16)
    part_out = jnp.dot(activation, grad_cells.T, preferred_element_type=jnp.float32)
    part_in = jnp.dot(normed, grad_pre.T, preferred_element_type=jnp.float32)
    grad_normed = jnp.dot(weight_in, grad_pre, preferred_element_type=jnp.float32)
    scaled_grad = grad_normed * norm_gain[:, None]
    mean_first = lax.optimization_barrier(jnp.sum(scaled_grad, axis=0)) / full_width
    mean_second = lax.optimization_barrier(jnp.sum(scaled_grad * centred, axis=0)) / full_width
    grad_conv = (inv_std * (scaled_grad - mean_first - centred * mean_second)).astype(jnp.bfloat16)
    return (branch, grad_conv, part_in, part_out)

def wrap_pad(array_f):
    rim_width = KW // 2
    wrapped = jnp.concatenate([array_f[:, :, -rim_width:], array_f, array_f[:, :, :rim_width]], axis=2)
    return jnp.pad(wrapped, ((0, 0), (rim_width, rim_width), (0, 0)))

def reference(ocean_state, sea_mask, kernel, conv_bias, norm_gain, norm_bias, weight_in, bias_in, weight_out, bias_out, layer_scale, cotangent):
    chan_count, row_count, lon_cells = ocean_state.shape
    state_f = ocean_state.astype(jnp.float32)
    padded = wrap_pad(state_f)
    conv_out = (depth_taps(padded, kernel, row_count, lon_cells) + conv_bias[:, None, None]).astype(jnp.bfloat16)
    mask_f = sea_mask.astype(jnp.float32)[None]
    grad_out = cotangent.astype(jnp.float32) * mask_f
    grad_branch = (grad_out * layer_scale[:, None, None]).astype(jnp.bfloat16)
    hid_count = weight_in.shape[1]

    def row_step(running, row_items):
        conv_row, grad_row = row_items
        branch, grad_conv, part_in, part_out = block_math(conv_row, grad_row, norm_gain, norm_bias, weight_in, bias_in, weight_out, bias_out)
        return ((running[0] + part_in, running[1] + part_out), (branch, grad_conv))
    zero_sums = (jnp.zeros((chan_count, hid_count), jnp.float32), jnp.zeros((hid_count, chan_count), jnp.float32))
    sums_out, rows_out = lax.scan(row_step, zero_sums, (jnp.transpose(conv_out, (1, 0, 2)), jnp.transpose(grad_branch, (1, 0, 2))))
    branch = jnp.transpose(rows_out[0], (1, 0, 2))
    grad_conv = jnp.transpose(rows_out[1], (1, 0, 2))
    updated = (mask_f * (state_f + layer_scale[:, None, None] * branch.astype(jnp.float32))).astype(jnp.bfloat16)
    padded_grad = wrap_pad(grad_conv.astype(jnp.float32))
    grad_state = (grad_out + depth_back(padded_grad, kernel, row_count, lon_cells)).astype(jnp.bfloat16)
    grad_scale = 1.0 / math.sqrt(row_count * lon_cells)
    return (updated, grad_state, sums_out[0] * grad_scale, sums_out[1] * grad_scale)
```

```python
import functools
import math

import jax
import jax.numpy as jnp
from jax import lax
from jax.experimental import pallas as pl
from jax.experimental.pallas import tpu as pltpu
from jax.sharding import PartitionSpec as P

KW = 7
RIM = KW // 2

root_coef = math.sqrt(2.0 / math.pi)
cubic_coef = 0.044715
norm_eps = 1e-06
VMEM_LIMIT = 56 * 1024 * 1024


def largest_divisor(n, bound):
    return max(d for d in range(1, bound + 1) if n % d == 0)


def rim_exchange(cells):
    count = lax.axis_size("lon")
    width = cells.shape[2]
    head = cells[:, :, :RIM]
    tail = cells[:, :, width - RIM :]
    left = lax.ppermute(tail, "lon", [(i, (i + 1) % count) for i in range(count)])
    right = lax.ppermute(head, "lon", [((i + 1) % count, i) for i in range(count)])
    gap = jnp.zeros(cells.shape[:2] + (width - 2 * RIM,), cells.dtype)
    return jnp.concatenate([right, gap, left], axis=2)


def tap_rows(kernel, row_count):
    taps = kernel.reshape(kernel.shape[0], KW, KW)
    return jnp.repeat(taps, row_count, axis=2)


def conv_channel(cells, rim, taps):
    row_count, width = cells.shape
    cells = cells.astype(jnp.float32)
    rim = rim.astype(jnp.float32)
    lane = lax.broadcasted_iota(jnp.int32, cells.shape, 1)
    shifted = []
    for b in range(KW):
        s = b - RIM
        if s == 0:
            moved = cells
        elif s > 0:
            moved = pltpu.roll(jnp.where(lane < s, rim, cells), width - s, 1)
        else:
            moved = pltpu.roll(jnp.where(lane >= width + s, rim, cells), -s, 1)
        shifted.append(moved.astype(jnp.bfloat16))
    shape = (row_count, KW * row_count)
    offset = (
        lax.rem(lax.broadcasted_iota(jnp.int32, shape, 1), row_count)
        - lax.broadcasted_iota(jnp.int32, shape, 0)
        + RIM
    )
    band = jnp.zeros(shape, jnp.float32)
    for a in range(KW):
        band = jnp.where(offset == a, taps[a : a + 1, :], band)
    return jnp.dot(
        band.astype(jnp.bfloat16),
        jnp.concatenate(shifted, axis=0),
        preferred_element_type=jnp.float32,
    )


def forward_kernel(block, state, rim, cot, mask, taps, bias, scale, conv_out, grad_branch):
    first = pl.program_id(0) * block
    mask_f = mask[...].astype(jnp.float32)

    def channel(k, carry):
        conv = conv_channel(state[k], rim[k], taps[k])
        conv_out[k] = (conv + bias[first + k]).astype(jnp.bfloat16)
        grad_out = cot[k].astype(jnp.float32) * mask_f
        grad_branch[k] = (grad_out * scale[first + k]).astype(jnp.bfloat16)
        return carry

    lax.fori_loop(0, block, channel, 0, unroll=2)


def backward_kernel(
    block, state, branch, grad_conv, rim, cot, mask, taps, scale, updated, grad_state
):
    first = pl.program_id(0) * block
    mask_f = mask[...].astype(jnp.float32)

    def channel(k, carry):
        conv = conv_channel(grad_conv[k], rim[k], taps[k])
        grad_out = cot[k].astype(jnp.float32) * mask_f
        grad_state[k] = (grad_out + conv).astype(jnp.bfloat16)
        value = state[k].astype(jnp.float32) + scale[first + k] * branch[k].astype(jnp.float32)
        updated[k] = (mask_f * value).astype(jnp.bfloat16)
        return carry

    lax.fori_loop(0, block, channel, 0, unroll=2)


def math_kernel(
    hid_block,
    conv_cells,
    grad_cells,
    gain,
    shift,
    win,
    win_t,
    bias_in,
    wout,
    wout_t,
    bias_out,
    branch,
    grad_conv,
    part_in,
    part_out,
    act,
    grad_pre,
):
    @pl.when(pl.program_id(0) == 0)
    def _():
        part_in[...] = jnp.zeros_like(part_in)
        part_out[...] = jnp.zeros_like(part_out)

    full_width = conv_cells.shape[0]
    values = conv_cells[...].astype(jnp.float32)
    mean_val = jnp.sum(values, axis=0, keepdims=True) / full_width
    square = jnp.sum(values * values, axis=0, keepdims=True) / full_width
    inv_std = lax.rsqrt(square - mean_val * mean_val + norm_eps)
    centred = (values - mean_val) * inv_std
    normed = (centred * gain[...] + shift[...]).astype(jnp.bfloat16)
    grads = grad_cells[...]
    across = (((1,), (1,)), ((), ()))
    for start in range(0, win_t.shape[0], hid_block):
        here = slice(start, start + hid_block)
        v = jnp.dot(win_t[here, :], normed, preferred_element_type=jnp.float32) + bias_in[here, :]
        tangent = jnp.tanh(root_coef * (v + cubic_coef * v * v * v))
        act_h = (0.5 * v * (1.0 + tangent)).astype(jnp.bfloat16)
        slope = 0.5 * (1.0 + tangent) + 0.5 * v * (1.0 - tangent * tangent) * root_coef * (
            1.0 + 3.0 * cubic_coef * v * v
        )
        grad_act = jnp.dot(wout[here, :], grads, preferred_element_type=jnp.float32)
        grad_h = (grad_act * slope).astype(jnp.bfloat16)
        act[here, :] = act_h
        grad_pre[here, :] = grad_h
        part_out[here, :] += lax.dot_general(
            act_h, grads, across, preferred_element_type=jnp.float32
        )
        part_in[here, :] += lax.dot_general(
            grad_h, normed, across, preferred_element_type=jnp.float32
        )
    branch[...] = (
        jnp.dot(wout_t[...], act[...], preferred_element_type=jnp.float32) + bias_out[...]
    ).astype(jnp.bfloat16)
    grad_normed = jnp.dot(win[...], grad_pre[...], preferred_element_type=jnp.float32)
    scaled_grad = grad_normed * gain[...]
    mean_first = jnp.sum(scaled_grad, axis=0, keepdims=True) / full_width
    mean_second = jnp.sum(scaled_grad * centred, axis=0, keepdims=True) / full_width
    grad_conv[...] = (inv_std * (scaled_grad - mean_first - centred * mean_second)).astype(
        jnp.bfloat16
    )


def block_math(conv_cells, grad_cells, gain, shift, win, bias_in, wout, bias_out):
    full_width, cells = conv_cells.shape
    hid = win.shape[1]
    block = largest_divisor(cells // 128, 2) * 128
    hid_block = 16 * largest_divisor(hid // 16, 20)
    tile = pl.BlockSpec((full_width, block), lambda i: (0, i))
    whole = lambda shape: pl.BlockSpec(shape, lambda i: (0, 0))
    bf16 = jnp.bfloat16
    part = jax.ShapeDtypeStruct((hid, full_width), jnp.float32)
    return pl.pallas_call(
        functools.partial(math_kernel, hid_block),
        grid=(cells // block,),
        in_specs=[
            tile,
            tile,
            whole((full_width, 1)),
            whole((full_width, 1)),
            whole((full_width, hid)),
            whole((hid, full_width)),
            whole((hid, 1)),
            whole((hid, full_width)),
            whole((full_width, hid)),
            whole((full_width, 1)),
        ],
        out_specs=[tile, tile, whole((hid, full_width)), whole((hid, full_width))],
        out_shape=[
            jax.ShapeDtypeStruct((full_width, cells), bf16),
            jax.ShapeDtypeStruct((full_width, cells), bf16),
            part,
            part,
        ],
        scratch_shapes=[pltpu.VMEM((hid, block), bf16), pltpu.VMEM((hid, block), bf16)],
        compiler_params=pltpu.CompilerParams(vmem_limit_bytes=VMEM_LIMIT),
        name="block_math",
    )(
        conv_cells,
        grad_cells,
        gain[:, None],
        shift[:, None],
        win,
        win.T,
        bias_in[:, None],
        wout,
        wout.T,
        bias_out[:, None],
    )


def body(
    ocean_state,
    sea_mask,
    kernel,
    conv_bias,
    norm_gain,
    norm_bias,
    weight_in,
    bias_in,
    weight_out,
    bias_out,
    layer_scale,
    cotangent,
):
    local_chan, row_count, lon_cells = ocean_state.shape
    chan_groups = lax.axis_size("ch")
    full_width = local_chan * chan_groups
    grad_scale = 1.0 / math.sqrt(row_count * lon_cells * lax.axis_size("lon"))
    block = largest_divisor(local_chan, 10)
    maps = pl.BlockSpec((block, row_count, lon_cells), lambda i: (i, 0, 0))
    one = pl.BlockSpec((row_count, lon_cells), lambda i: (0, 0))
    rows = pl.BlockSpec((block, KW, KW * row_count), lambda i: (i, 0, 0))
    scalars = pl.BlockSpec(memory_space=pltpu.SMEM)
    like = jax.ShapeDtypeStruct(ocean_state.shape, jnp.bfloat16)
    params = pltpu.CompilerParams(vmem_limit_bytes=VMEM_LIMIT)

    conv_out, grad_branch = pl.pallas_call(
        functools.partial(forward_kernel, block),
        grid=(local_chan // block,),
        in_specs=[maps, maps, maps, one, rows, scalars, scalars],
        out_specs=[maps, maps],
        out_shape=[like, like],
        compiler_params=params,
        name="forward_conv",
    )(
        ocean_state,
        rim_exchange(ocean_state),
        cotangent,
        sea_mask,
        tap_rows(kernel, row_count),
        conv_bias,
        layer_scale,
    )
    quarter = row_count // chan_groups
    conv_cells, grad_cells = (
        lax.all_to_all(conv_out, "ch", split_axis=1, concat_axis=0, tiled=True),
        lax.all_to_all(grad_branch, "ch", split_axis=1, concat_axis=0, tiled=True),
    )
    branch_cells, conv_grad_cells, part_in, part_out = block_math(
        conv_cells.reshape(full_width, quarter * lon_cells),
        grad_cells.reshape(full_width, quarter * lon_cells),
        norm_gain,
        norm_bias,
        weight_in,
        bias_in,
        weight_out,
        bias_out,
    )
    sum_in, sum_out = lax.psum((part_in, part_out), ("lon", "ch"))
    branch, grad_conv = (
        lax.all_to_all(
            cells.reshape(full_width, quarter, lon_cells),
            "ch",
            split_axis=0,
            concat_axis=1,
            tiled=True,
        )
        for cells in (branch_cells, conv_grad_cells)
    )
    updated, grad_state = pl.pallas_call(
        functools.partial(backward_kernel, block),
        grid=(local_chan // block,),
        in_specs=[maps, maps, maps, maps, maps, one, rows, scalars],
        out_specs=[maps, maps],
        out_shape=[like, like],
        compiler_params=params,
        name="backward_conv",
    )(
        ocean_state,
        branch,
        grad_conv,
        rim_exchange(grad_conv),
        cotangent,
        sea_mask,
        tap_rows(kernel[:, ::-1], row_count),
        layer_scale,
    )
    return (updated, grad_state, sum_in.T * grad_scale, sum_out * grad_scale)


def solution(mesh):
    return jax.shard_map(
        body,
        mesh=mesh,
        in_specs=(
            P("ch", None, "lon"),
            P(None, "lon"),
            P("ch", None),
            P("ch"),
            P(),
            P(),
            P(),
            P(),
            P(),
            P(),
            P("ch"),
            P("ch", None, "lon"),
        ),
        out_specs=(P("ch", None, "lon"), P("ch", None, "lon"), P(), P()),
        check_vma=False,
    )
```

```python
import functools
import math

import jax
import jax.numpy as jnp
from jax import lax
from jax.experimental import pallas as pl
from jax.experimental.pallas import tpu as pltpu
from jax.sharding import PartitionSpec as P

KW = 7
RIM = KW // 2

root_coef = math.sqrt(2.0 / math.pi)
cubic_coef = 0.044715
norm_eps = 1e-06
VMEM_LIMIT = 56 * 1024 * 1024


def largest_divisor(n, bound):
    return max(d for d in range(1, bound + 1) if n % d == 0)


def rim_exchange(cells):
    count = lax.axis_size("lon")
    width = cells.shape[2]
    head = cells[:, :, :RIM]
    tail = cells[:, :, width - RIM :]
    left = lax.ppermute(tail, "lon", [(i, (i + 1) % count) for i in range(count)])
    right = lax.ppermute(head, "lon", [((i + 1) % count, i) for i in range(count)])
    gap = jnp.zeros(cells.shape[:2] + (width - 2 * RIM,), cells.dtype)
    return jnp.concatenate([right, gap, left], axis=2)


def tap_rows(kernel, row_count):
    taps = kernel.reshape(kernel.shape[0], KW, KW)
    return jnp.repeat(taps, row_count, axis=2)


def conv_channel(cells, rim, taps):
    row_count, width = cells.shape
    cells = cells.astype(jnp.float32)
    rim = rim.astype(jnp.float32)
    lane = lax.broadcasted_iota(jnp.int32, cells.shape, 1)
    shifted = []
    for b in range(KW):
        s = b - RIM
        if s == 0:
            moved = cells
        elif s > 0:
            moved = pltpu.roll(jnp.where(lane < s, rim, cells), width - s, 1)
        else:
            moved = pltpu.roll(jnp.where(lane >= width + s, rim, cells), -s, 1)
        shifted.append(moved.astype(jnp.bfloat16))
    shape = (row_count, KW * row_count)
    offset = (
        lax.rem(lax.broadcasted_iota(jnp.int32, shape, 1), row_count)
        - lax.broadcasted_iota(jnp.int32, shape, 0)
        + RIM
    )
    band = jnp.zeros(shape, jnp.float32)
    for a in range(KW):
        band = jnp.where(offset == a, taps[a : a + 1, :], band)
    return jnp.dot(
        band.astype(jnp.bfloat16),
        jnp.concatenate(shifted, axis=0),
        preferred_element_type=jnp.float32,
    )


def greet_peers(peers):
    me = lax.axis_index("ch")
    barrier = pltpu.get_barrier_semaphore()
    for r in range(1, peers):
        pl.semaphore_signal(
            barrier,
            inc=1,
            device_id={"ch": lax.rem(me + r, peers)},
            device_id_type=pl.DeviceIdType.MESH,
        )
    pl.semaphore_wait(barrier, peers - 1)


def forward_kernel(
    block,
    peers,
    state,
    rim,
    cot,
    mask,
    taps,
    bias,
    scale,
    conv_cells,
    grad_cells,
    conv_out,
    grad_branch,
    send_sem,
    recv_sem,
    own_sem,
):
    step = pl.program_id(0)
    steps = pl.num_programs(0)
    first = step * block
    me = lax.axis_index("ch")
    local_chan, row_count, _ = conv_out.shape
    quarter = row_count // peers
    pairs = ((conv_out, conv_cells), (grad_branch, grad_cells))

    def views(which, at, target):
        source, sink = pairs[which]
        rows = pl.ds(pl.multiple_of(target * quarter, quarter), quarter)
        return (
            source.at[pl.ds(at * block, block), rows, :],
            sink.at[pl.ds(me * local_chan + at * block, block)],
        )

    def remote(which, at, r):
        target = lax.rem(me + r, peers)
        source, sink = views(which, at, target)
        return pltpu.make_async_remote_copy(
            src_ref=source,
            dst_ref=sink,
            send_sem=send_sem.at[which, at, r - 1],
            recv_sem=recv_sem.at[which, at, r - 1],
            device_id={"ch": target},
            device_id_type=pl.DeviceIdType.MESH,
        )

    def own(which, at):
        source, sink = views(which, at, me)
        return pltpu.make_async_copy(source, sink, own_sem.at[which, at])

    @pl.when(step == 0)
    def _():
        greet_peers(peers)

    mask_f = mask[...].astype(jnp.float32)

    def channel(k, carry):
        conv = conv_channel(state[k], rim[k], taps[k])
        conv_out[first + k] = (conv + bias[first + k]).astype(jnp.bfloat16)
        grad_out = cot[k].astype(jnp.float32) * mask_f
        grad_branch[first + k] = (grad_out * scale[first + k]).astype(jnp.bfloat16)
        return carry

    lax.fori_loop(0, block, channel, 0, unroll=2)
    for which in range(2):
        for r in range(1, peers):
            remote(which, step, r).start()
        own(which, step).start()

    @pl.when(step == steps - 1)
    def _():
        def finish(at, carry):
            for which in range(2):
                for r in range(1, peers):
                    remote(which, at, r).wait()
                own(which, at).wait()
            return carry

        lax.fori_loop(0, steps, finish, 0)


def return_kernel(
    peers, branch_cells, grad_cells, branch, grad_conv, send_sem, recv_sem, own_sem
):
    me = lax.axis_index("ch")
    local_chan, row_count, _ = branch.shape
    quarter = row_count // peers
    mine = pl.ds(pl.multiple_of(me * quarter, quarter), quarter)
    greet_peers(peers)
    copies = []
    for which, (source, sink) in enumerate(((grad_cells, grad_conv), (branch_cells, branch))):
        for r in range(1, peers):
            target = lax.rem(me + r, peers)
            copies.append(
                pltpu.make_async_remote_copy(
                    src_ref=source.at[pl.ds(target * local_chan, local_chan)],
                    dst_ref=sink.at[:, mine, :],
                    send_sem=send_sem.at[which, r - 1],
                    recv_sem=recv_sem.at[which, r - 1],
                    device_id={"ch": target},
                    device_id_type=pl.DeviceIdType.MESH,
                )
            )
        copies.append(
            pltpu.make_async_copy(
                source.at[pl.ds(me * local_chan, local_chan)],
                sink.at[:, mine, :],
                own_sem.at[which],
            )
        )
    for copy in copies:
        copy.start()
    for copy in copies:
        copy.wait()


def backward_kernel(
    block, state, branch, grad_conv, rim, cot, mask, taps, scale, updated, grad_state
):
    first = pl.program_id(0) * block
    mask_f = mask[...].astype(jnp.float32)

    def channel(k, carry):
        conv = conv_channel(grad_conv[k], rim[k], taps[k])
        grad_out = cot[k].astype(jnp.float32) * mask_f
        grad_state[k] = (grad_out + conv).astype(jnp.bfloat16)
        value = state[k].astype(jnp.float32) + scale[first + k] * branch[k].astype(jnp.float32)
        updated[k] = (mask_f * value).astype(jnp.bfloat16)
        return carry

    lax.fori_loop(0, block, channel, 0, unroll=2)


def math_kernel(
    hid_block,
    conv_cells,
    grad_cells,
    gain,
    shift,
    win,
    win_t,
    bias_in,
    wout,
    wout_t,
    bias_out,
    branch,
    grad_conv,
    in_total,
    out_total,
    act,
    grad_pre,
    part_in,
    part_out,
):
    @pl.when(pl.program_id(0) == 0)
    def _():
        part_in[...] = jnp.zeros_like(part_in)
        part_out[...] = jnp.zeros_like(part_out)

    full_width = conv_cells.shape[0]
    values = conv_cells[...].astype(jnp.float32)
    mean_val = jnp.sum(values, axis=0, keepdims=True) / full_width
    square = jnp.sum(values * values, axis=0, keepdims=True) / full_width
    inv_std = lax.rsqrt(square - mean_val * mean_val + norm_eps)
    centred = (values - mean_val) * inv_std
    normed = (centred * gain[...] + shift[...]).astype(jnp.bfloat16)
    grads = grad_cells[...]
    across = (((1,), (1,)), ((), ()))
    for start in range(0, win_t.shape[0], hid_block):
        here = slice(start, start + hid_block)
        v = jnp.dot(win_t[here, :], normed, preferred_element_type=jnp.float32) + bias_in[here, :]
        tangent = jnp.tanh(root_coef * (v + cubic_coef * v * v * v))
        act_h = (0.5 * v * (1.0 + tangent)).astype(jnp.bfloat16)
        slope = 0.5 * (1.0 + tangent) + 0.5 * v * (1.0 - tangent * tangent) * root_coef * (
            1.0 + 3.0 * cubic_coef * v * v
        )
        grad_act = jnp.dot(wout[here, :], grads, preferred_element_type=jnp.float32)
        grad_h = (grad_act * slope).astype(jnp.bfloat16)
        act[here, :] = act_h
        grad_pre[here, :] = grad_h
        part_out[here, :] += lax.dot_general(
            act_h, grads, across, preferred_element_type=jnp.float32
        )
        part_in[here, :] += lax.dot_general(
            grad_h, normed, across, preferred_element_type=jnp.float32
        )
    branch[...] = (
        jnp.dot(wout_t[...], act[...], preferred_element_type=jnp.float32) + bias_out[...]
    ).astype(jnp.bfloat16)
    grad_normed = jnp.dot(win[...], grad_pre[...], preferred_element_type=jnp.float32)
    scaled_grad = grad_normed * gain[...]
    mean_first = jnp.sum(scaled_grad, axis=0, keepdims=True) / full_width
    mean_second = jnp.sum(scaled_grad * centred, axis=0, keepdims=True) / full_width
    grad_conv[...] = (inv_std * (scaled_grad - mean_first - centred * mean_second)).astype(
        jnp.bfloat16
    )

    @pl.when(pl.program_id(0) == pl.num_programs(0) - 1)
    def _():
        in_total[...] = part_in[...].astype(jnp.bfloat16)
        out_total[...] = part_out[...].astype(jnp.bfloat16)


def block_math(conv_cells, grad_cells, gain, shift, win, bias_in, wout, bias_out):
    full_width, cells = conv_cells.shape
    hid = win.shape[1]
    block = largest_divisor(cells // 128, 2) * 128
    hid_block = 16 * largest_divisor(hid // 16, 20)
    tile = pl.BlockSpec((full_width, block), lambda i: (0, i))
    whole = lambda shape: pl.BlockSpec(shape, lambda i: (0, 0))
    bf16 = jnp.bfloat16
    part = jax.ShapeDtypeStruct((hid, full_width), bf16)
    return pl.pallas_call(
        functools.partial(math_kernel, hid_block),
        grid=(cells // block,),
        in_specs=[
            tile,
            tile,
            whole((full_width, 1)),
            whole((full_width, 1)),
            whole((full_width, hid)),
            whole((hid, full_width)),
            whole((hid, 1)),
            whole((hid, full_width)),
            whole((full_width, hid)),
            whole((full_width, 1)),
        ],
        out_specs=[tile, tile, whole((hid, full_width)), whole((hid, full_width))],
        out_shape=[
            jax.ShapeDtypeStruct((full_width, cells), bf16),
            jax.ShapeDtypeStruct((full_width, cells), bf16),
            part,
            part,
        ],
        scratch_shapes=[
            pltpu.VMEM((hid, block), bf16),
            pltpu.VMEM((hid, block), bf16),
            pltpu.VMEM((hid, full_width), jnp.float32),
            pltpu.VMEM((hid, full_width), jnp.float32),
        ],
        compiler_params=pltpu.CompilerParams(vmem_limit_bytes=VMEM_LIMIT),
        name="block_math",
    )(
        conv_cells,
        grad_cells,
        gain[:, None],
        shift[:, None],
        win,
        win.T,
        bias_in[:, None],
        wout,
        wout.T,
        bias_out[:, None],
    )


def body(
    ocean_state,
    sea_mask,
    kernel,
    conv_bias,
    norm_gain,
    norm_bias,
    weight_in,
    bias_in,
    weight_out,
    bias_out,
    layer_scale,
    cotangent,
):
    local_chan, row_count, lon_cells = ocean_state.shape
    chan_groups = lax.axis_size("ch")
    full_width = local_chan * chan_groups
    grad_scale = 1.0 / math.sqrt(row_count * lon_cells * lax.axis_size("lon"))
    block = largest_divisor(local_chan, 10)
    maps = pl.BlockSpec((block, row_count, lon_cells), lambda i: (i, 0, 0))
    one = pl.BlockSpec((row_count, lon_cells), lambda i: (0, 0))
    rows = pl.BlockSpec((block, KW, KW * row_count), lambda i: (i, 0, 0))
    scalars = pl.BlockSpec(memory_space=pltpu.SMEM)
    like = jax.ShapeDtypeStruct(ocean_state.shape, jnp.bfloat16)
    params = pltpu.CompilerParams(vmem_limit_bytes=VMEM_LIMIT)

    quarter = row_count // chan_groups
    steps = local_chan // block
    shares = jax.ShapeDtypeStruct((full_width, quarter, lon_cells), jnp.bfloat16)
    anywhere = pl.BlockSpec(memory_space=pl.ANY)
    conv_cells, grad_cells = pl.pallas_call(
        functools.partial(forward_kernel, block, chan_groups),
        grid=(steps,),
        in_specs=[maps, maps, maps, one, rows, scalars, scalars],
        out_specs=[anywhere, anywhere],
        out_shape=[shares, shares],
        scratch_shapes=[
            pltpu.VMEM(ocean_state.shape, jnp.bfloat16),
            pltpu.VMEM(ocean_state.shape, jnp.bfloat16),
            pltpu.SemaphoreType.DMA((2, steps, chan_groups - 1)),
            pltpu.SemaphoreType.DMA((2, steps, chan_groups - 1)),
            pltpu.SemaphoreType.DMA((2, steps)),
        ],
        compiler_params=pltpu.CompilerParams(
            vmem_limit_bytes=VMEM_LIMIT, collective_id=0, has_side_effects=True
        ),
        name="forward_conv",
    )(
        ocean_state,
        rim_exchange(ocean_state),
        cotangent,
        sea_mask,
        tap_rows(kernel, row_count),
        conv_bias,
        layer_scale,
    )
    branch_cells, conv_grad_cells, part_in, part_out = block_math(
        conv_cells.reshape(full_width, quarter * lon_cells),
        grad_cells.reshape(full_width, quarter * lon_cells),
        norm_gain,
        norm_bias,
        weight_in,
        bias_in,
        weight_out,
        bias_out,
    )
    sum_in, sum_out = lax.psum((part_in, part_out), ("lon", "ch"))
    branch, grad_conv = pl.pallas_call(
        functools.partial(return_kernel, chan_groups),
        in_specs=[anywhere, anywhere],
        out_specs=[anywhere, anywhere],
        out_shape=[like, like],
        scratch_shapes=[
            pltpu.SemaphoreType.DMA((2, chan_groups - 1)),
            pltpu.SemaphoreType.DMA((2, chan_groups - 1)),
            pltpu.SemaphoreType.DMA((2,)),
        ],
        compiler_params=pltpu.CompilerParams(collective_id=1, has_side_effects=True),
        cost_estimate=pl.CostEstimate(flops=0, bytes_accessed=1, transcendentals=0),
        name="return_cells",
    )(
        branch_cells.reshape(shares.shape),
        conv_grad_cells.reshape(shares.shape),
    )
    updated, grad_state = pl.pallas_call(
        functools.partial(backward_kernel, block),
        grid=(local_chan // block,),
        in_specs=[maps, maps, maps, maps, maps, one, rows, scalars],
        out_specs=[maps, maps],
        out_shape=[like, like],
        compiler_params=params,
        cost_estimate=pl.CostEstimate(flops=0, bytes_accessed=1, transcendentals=0),
        name="backward_conv",
    )(
        ocean_state,
        branch,
        grad_conv,
        rim_exchange(grad_conv),
        cotangent,
        sea_mask,
        tap_rows(kernel[:, ::-1], row_count),
        layer_scale,
    )
    return (
        updated,
        grad_state,
        sum_in.T.astype(jnp.float32) * grad_scale,
        sum_out.astype(jnp.float32) * grad_scale,
    )


def solution(mesh):
    return jax.shard_map(
        body,
        mesh=mesh,
        in_specs=(
            P("ch", None, "lon"),
            P(None, "lon"),
            P("ch", None),
            P("ch"),
            P(),
            P(),
            P(),
            P(),
            P(),
            P(),
            P("ch"),
            P("ch", None, "lon"),
        ),
        out_specs=(P("ch", None, "lon"), P("ch", None, "lon"), P(), P()),
        check_vma=False,
    )
```

```python
import functools
import math

import jax
import jax.numpy as jnp
from jax import lax
from jax.experimental import pallas as pl
from jax.experimental.pallas import tpu as pltpu
from jax.sharding import PartitionSpec as P

KW = 7
RIM = KW // 2

root_coef = math.sqrt(2.0 / math.pi)
cubic_coef = 0.044715
norm_eps = 1e-06
VMEM_LIMIT = 56 * 1024 * 1024


def largest_divisor(n, bound):
    return max(d for d in range(1, bound + 1) if n % d == 0)


def rim_exchange(cells):
    count = lax.axis_size("lon")
    width = cells.shape[2]
    head = cells[:, :, :RIM]
    tail = cells[:, :, width - RIM :]
    left = lax.ppermute(tail, "lon", [(i, (i + 1) % count) for i in range(count)])
    right = lax.ppermute(head, "lon", [((i + 1) % count, i) for i in range(count)])
    gap = jnp.zeros(cells.shape[:2] + (width - 2 * RIM,), cells.dtype)
    return jnp.concatenate([right, gap, left], axis=2)


def tap_rows(kernel, row_count):
    taps = kernel.reshape(kernel.shape[0], KW, KW)
    return jnp.repeat(taps, row_count, axis=2)


def conv_channel(cells, rim, taps):
    row_count, width = cells.shape
    cells = cells.astype(jnp.float32)
    rim = rim.astype(jnp.float32)
    lane = lax.broadcasted_iota(jnp.int32, cells.shape, 1)
    shifted = []
    for b in range(KW):
        s = b - RIM
        if s == 0:
            moved = cells
        elif s > 0:
            moved = pltpu.roll(jnp.where(lane < s, rim, cells), width - s, 1)
        else:
            moved = pltpu.roll(jnp.where(lane >= width + s, rim, cells), -s, 1)
        shifted.append(moved.astype(jnp.bfloat16))
    shape = (row_count, KW * row_count)
    offset = (
        lax.rem(lax.broadcasted_iota(jnp.int32, shape, 1), row_count)
        - lax.broadcasted_iota(jnp.int32, shape, 0)
        + RIM
    )
    band = jnp.zeros(shape, jnp.float32)
    for a in range(KW):
        band = jnp.where(offset == a, taps[a : a + 1, :], band)
    return jnp.dot(
        band.astype(jnp.bfloat16),
        jnp.concatenate(shifted, axis=0),
        preferred_element_type=jnp.float32,
    )


def greet_peers(peers):
    me = lax.axis_index("ch")
    barrier = pltpu.get_barrier_semaphore()
    for r in range(1, peers):
        pl.semaphore_signal(
            barrier,
            inc=1,
            device_id={"ch": lax.rem(me + r, peers)},
            device_id_type=pl.DeviceIdType.MESH,
        )
    pl.semaphore_wait(barrier, peers - 1)


def forward_kernel(
    block,
    peers,
    state,
    rim,
    cot,
    mask,
    taps,
    bias,
    scale,
    conv_cells,
    grad_cells,
    conv_out,
    grad_branch,
    send_sem,
    recv_sem,
    own_sem,
):
    step = pl.program_id(0)
    steps = pl.num_programs(0)
    first = step * block
    me = lax.axis_index("ch")
    local_chan, row_count, _ = conv_out.shape
    quarter = row_count // peers
    pairs = ((conv_out, conv_cells), (grad_branch, grad_cells))

    def views(which, at, target):
        source, sink = pairs[which]
        rows = pl.ds(pl.multiple_of(target * quarter, quarter), quarter)
        return (
            source.at[pl.ds(at * block, block), rows, :],
            sink.at[pl.ds(me * local_chan + at * block, block)],
        )

    def remote(which, at, r):
        target = lax.rem(me + r, peers)
        source, sink = views(which, at, target)
        return pltpu.make_async_remote_copy(
            src_ref=source,
            dst_ref=sink,
            send_sem=send_sem.at[which, at, r - 1],
            recv_sem=recv_sem.at[which, at, r - 1],
            device_id={"ch": target},
            device_id_type=pl.DeviceIdType.MESH,
        )

    def own(which, at):
        source, sink = views(which, at, me)
        return pltpu.make_async_copy(source, sink, own_sem.at[which, at])

    @pl.when(step == 0)
    def _():
        greet_peers(peers)

    mask_f = mask[...].astype(jnp.float32)

    def channel(k, carry):
        conv = conv_channel(state[k], rim[k], taps[k])
        conv_out[first + k] = (conv + bias[first + k]).astype(jnp.bfloat16)
        grad_out = cot[k].astype(jnp.float32) * mask_f
        grad_branch[first + k] = (grad_out * scale[first + k]).astype(jnp.bfloat16)
        return carry

    lax.fori_loop(0, block, channel, 0, unroll=2)
    for which in range(2):
        for r in range(1, peers):
            remote(which, step, r).start()
        own(which, step).start()

    @pl.when(step == steps - 1)
    def _():
        def finish(at, carry):
            for which in range(2):
                for r in range(1, peers):
                    remote(which, at, r).wait()
                own(which, at).wait()
            return carry

        lax.fori_loop(0, steps, finish, 0)


def backward_kernel(
    block, state, branch, grad_conv, rim, cot, mask, taps, scale, updated, grad_state
):
    first = pl.program_id(0) * block
    mask_f = mask[...].astype(jnp.float32)

    def channel(k, carry):
        conv = conv_channel(grad_conv[k], rim[k], taps[k])
        grad_out = cot[k].astype(jnp.float32) * mask_f
        grad_state[k] = (grad_out + conv).astype(jnp.bfloat16)
        value = state[k].astype(jnp.float32) + scale[first + k] * branch[k].astype(jnp.float32)
        updated[k] = (mask_f * value).astype(jnp.bfloat16)
        return carry

    lax.fori_loop(0, block, channel, 0, unroll=2)


def math_kernel(
    hid_block,
    peers,
    conv_cells,
    grad_cells,
    gain,
    shift,
    win,
    win_t,
    bias_in,
    wout,
    wout_t,
    bias_out,
    branch,
    grad_conv,
    in_total,
    out_total,
    act,
    grad_pre,
    part_in,
    part_out,
    spread,
    outgoing,
    send_sem,
    recv_sem,
    own_sem,
):
    step = pl.program_id(0)
    steps = pl.num_programs(0)
    me = lax.axis_index("ch")
    full_width, block = conv_cells.shape
    hid = win.shape[1]
    local_chan = full_width // peers
    padded = branch.shape[0]
    sinks = (branch, grad_conv)

    def views(which, at, target):
        start = pl.multiple_of(me * (steps * block) + at * block, 128)
        return (
            outgoing.at[which, at, pl.ds(pl.multiple_of(target * padded, 16), padded), :],
            sinks[which].at[:, pl.ds(start, block)],
        )

    def remote(which, at, r):
        target = lax.rem(me + r, peers)
        source, sink = views(which, at, target)
        return pltpu.make_async_remote_copy(
            src_ref=source,
            dst_ref=sink,
            send_sem=send_sem.at[which, at, r - 1],
            recv_sem=recv_sem.at[which, at, r - 1],
            device_id={"ch": target},
            device_id_type=pl.DeviceIdType.MESH,
        )

    def own(which, at):
        source, sink = views(which, at, me)
        return pltpu.make_async_copy(source, sink, own_sem.at[which, at])

    def send(which, cells):
        for g in range(peers):
            spread[g * padded : g * padded + local_chan, :] = cells[
                g * local_chan : (g + 1) * local_chan, :
            ]
        outgoing[which, step] = spread[...].astype(jnp.bfloat16)
        for r in range(1, peers):
            remote(which, step, r).start()
        own(which, step).start()

    @pl.when(step == 0)
    def _():
        greet_peers(peers)
        part_in[...] = jnp.zeros_like(part_in)
        part_out[...] = jnp.zeros_like(part_out)
        spread[...] = jnp.zeros_like(spread)

    values = conv_cells[...].astype(jnp.float32)
    mean_val = jnp.sum(values, axis=0, keepdims=True) / full_width
    square = jnp.sum(values * values, axis=0, keepdims=True) / full_width
    inv_std = lax.rsqrt(square - mean_val * mean_val + norm_eps)
    centred = (values - mean_val) * inv_std
    normed = (centred * gain[...] + shift[...]).astype(jnp.bfloat16)
    grads = grad_cells[...]
    across = (((1,), (1,)), ((), ()))
    for start in range(0, hid, hid_block):
        here = slice(start, min(start + hid_block, hid))
        v = jnp.dot(win_t[here, :], normed, preferred_element_type=jnp.float32) + bias_in[here, :]
        tangent = jnp.tanh(root_coef * (v + cubic_coef * v * v * v))
        act_h = (0.5 * v * (1.0 + tangent)).astype(jnp.bfloat16)
        slope = 0.5 * (1.0 + tangent) + 0.5 * v * (1.0 - tangent * tangent) * root_coef * (
            1.0 + 3.0 * cubic_coef * v * v
        )
        grad_act = jnp.dot(wout[here, :], grads, preferred_element_type=jnp.float32)
        grad_h = (grad_act * slope).astype(jnp.bfloat16)
        act[here, :] = act_h
        grad_pre[here, :] = grad_h
        part_out[:, here] += lax.dot_general(
            grads, act_h, across, preferred_element_type=jnp.float32
        )
        part_in[:, here] += lax.dot_general(
            normed, grad_h, across, preferred_element_type=jnp.float32
        )
    grad_normed = jnp.dot(win[...], grad_pre[...], preferred_element_type=jnp.float32)
    scaled_grad = grad_normed * gain[...]
    mean_first = jnp.sum(scaled_grad, axis=0, keepdims=True) / full_width
    mean_second = jnp.sum(scaled_grad * centred, axis=0, keepdims=True) / full_width
    send(1, inv_std * (scaled_grad - mean_first - centred * mean_second))
    send(0, jnp.dot(wout_t[...], act[...], preferred_element_type=jnp.float32) + bias_out[...])

    @pl.when(step == steps - 1)
    def _():
        in_total[...] = part_in[...].astype(jnp.bfloat16)
        out_total[...] = part_out[...].astype(jnp.bfloat16)

        def finish(at, carry):
            for which in range(2):
                for r in range(1, peers):
                    remote(which, at, r).wait()
                own(which, at).wait()
            return carry

        lax.fori_loop(0, steps, finish, 0)


def block_math(conv_cells, grad_cells, gain, shift, win, bias_in, wout, bias_out):
    full_width, cells = conv_cells.shape
    hid = win.shape[1]
    peers = lax.axis_size("ch")
    padded = -(-(full_width // peers) // 16) * 16
    block = largest_divisor(cells // 128, 2) * 128
    steps = cells // block
    hid_block = 5 * 128
    tile = pl.BlockSpec((full_width, block), lambda i: (0, i))
    whole = lambda shape: pl.BlockSpec(shape, lambda i: (0, 0))
    anywhere = pl.BlockSpec(memory_space=pl.ANY)
    bf16 = jnp.bfloat16
    part = jax.ShapeDtypeStruct((full_width, hid), bf16)
    back = jax.ShapeDtypeStruct((padded, peers * cells), bf16)
    return pl.pallas_call(
        functools.partial(math_kernel, hid_block, peers),
        grid=(steps,),
        in_specs=[
            tile,
            tile,
            whole((full_width, 1)),
            whole((full_width, 1)),
            whole((full_width, hid)),
            whole((hid, full_width)),
            whole((hid, 1)),
            whole((hid, full_width)),
            whole((full_width, hid)),
            whole((full_width, 1)),
        ],
        out_specs=[anywhere, anywhere, whole((full_width, hid)), whole((full_width, hid))],
        out_shape=[back, back, part, part],
        scratch_shapes=[
            pltpu.VMEM((hid, block), bf16),
            pltpu.VMEM((hid, block), bf16),
            pltpu.VMEM((full_width, hid), jnp.float32),
            pltpu.VMEM((full_width, hid), jnp.float32),
            pltpu.VMEM((peers * padded, block), jnp.float32),
            pltpu.VMEM((2, steps, peers * padded, block), bf16),
            pltpu.SemaphoreType.DMA((2, steps, peers - 1)),
            pltpu.SemaphoreType.DMA((2, steps, peers - 1)),
            pltpu.SemaphoreType.DMA((2, steps)),
        ],
        compiler_params=pltpu.CompilerParams(
            vmem_limit_bytes=VMEM_LIMIT, collective_id=1, has_side_effects=True
        ),
        name="block_math",
    )(
        conv_cells,
        grad_cells,
        gain[:, None],
        shift[:, None],
        win,
        win.T,
        bias_in[:, None],
        wout,
        wout.T,
        bias_out[:, None],
    )


def body(
    ocean_state,
    sea_mask,
    kernel,
    conv_bias,
    norm_gain,
    norm_bias,
    weight_in,
    bias_in,
    weight_out,
    bias_out,
    layer_scale,
    cotangent,
):
    local_chan, row_count, lon_cells = ocean_state.shape
    chan_groups = lax.axis_size("ch")
    full_width = local_chan * chan_groups
    grad_scale = 1.0 / math.sqrt(row_count * lon_cells * lax.axis_size("lon"))
    block = largest_divisor(local_chan, 10)
    maps = pl.BlockSpec((block, row_count, lon_cells), lambda i: (i, 0, 0))
    one = pl.BlockSpec((row_count, lon_cells), lambda i: (0, 0))
    rows = pl.BlockSpec((block, KW, KW * row_count), lambda i: (i, 0, 0))
    scalars = pl.BlockSpec(memory_space=pltpu.SMEM)
    like = jax.ShapeDtypeStruct(ocean_state.shape, jnp.bfloat16)
    params = pltpu.CompilerParams(vmem_limit_bytes=VMEM_LIMIT)

    quarter = row_count // chan_groups
    steps = local_chan // block
    shares = jax.ShapeDtypeStruct((full_width, quarter, lon_cells), jnp.bfloat16)
    anywhere = pl.BlockSpec(memory_space=pl.ANY)
    conv_cells, grad_cells = pl.pallas_call(
        functools.partial(forward_kernel, block, chan_groups),
        grid=(steps,),
        in_specs=[maps, maps, maps, one, rows, scalars, scalars],
        out_specs=[anywhere, anywhere],
        out_shape=[shares, shares],
        scratch_shapes=[
            pltpu.VMEM(ocean_state.shape, jnp.bfloat16),
            pltpu.VMEM(ocean_state.shape, jnp.bfloat16),
            pltpu.SemaphoreType.DMA((2, steps, chan_groups - 1)),
            pltpu.SemaphoreType.DMA((2, steps, chan_groups - 1)),
            pltpu.SemaphoreType.DMA((2, steps)),
        ],
        compiler_params=pltpu.CompilerParams(
            vmem_limit_bytes=VMEM_LIMIT, collective_id=0, has_side_effects=True
        ),
        name="forward_conv",
    )(
        ocean_state,
        rim_exchange(ocean_state),
        cotangent,
        sea_mask,
        tap_rows(kernel, row_count),
        conv_bias,
        layer_scale,
    )
    branch, grad_conv, part_in, part_out = block_math(
        conv_cells.reshape(full_width, quarter * lon_cells),
        grad_cells.reshape(full_width, quarter * lon_cells),
        norm_gain,
        norm_bias,
        weight_in,
        bias_in,
        weight_out,
        bias_out,
    )
    sum_in, sum_out = lax.psum((part_in, part_out), ("lon", "ch"))
    branch, grad_conv = (
        cells[:local_chan].reshape(ocean_state.shape) for cells in (branch, grad_conv)
    )
    updated, grad_state = pl.pallas_call(
        functools.partial(backward_kernel, block),
        grid=(local_chan // block,),
        in_specs=[maps, maps, maps, maps, maps, one, rows, scalars],
        out_specs=[maps, maps],
        out_shape=[like, like],
        compiler_params=params,
        cost_estimate=pl.CostEstimate(flops=0, bytes_accessed=1, transcendentals=0),
        name="backward_conv",
    )(
        ocean_state,
        branch,
        grad_conv,
        rim_exchange(grad_conv),
        cotangent,
        sea_mask,
        tap_rows(kernel[:, ::-1], row_count),
        layer_scale,
    )
    return (
        updated,
        grad_state,
        sum_in.astype(jnp.float32) * grad_scale,
        sum_out.T.astype(jnp.float32) * grad_scale,
    )


def solution(mesh):
    return jax.shard_map(
        body,
        mesh=mesh,
        in_specs=(
            P("ch", None, "lon"),
            P(None, "lon"),
            P("ch", None),
            P("ch"),
            P(),
            P(),
            P(),
            P(),
            P(),
            P(),
            P("ch"),
            P("ch", None, "lon"),
        ),
        out_specs=(P("ch", None, "lon"), P("ch", None, "lon"), P(), P()),
        check_vma=False,
    )
```

```python
import functools
import math

import jax
import jax.numpy as jnp
from jax import lax
from jax.experimental import pallas as pl
from jax.experimental.pallas import tpu as pltpu
from jax.sharding import PartitionSpec as P

KW = 7
RIM = KW // 2

root_coef = math.sqrt(2.0 / math.pi)
cubic_coef = 0.044715
norm_eps = 1e-06
VMEM_LIMIT = 56 * 1024 * 1024


def largest_divisor(n, bound):
    return max(d for d in range(1, bound + 1) if n % d == 0)


def rim_exchange(cells):
    count = lax.axis_size("lon")
    width = cells.shape[2]
    head = cells[:, :, :RIM]
    tail = cells[:, :, width - RIM :]
    left = lax.ppermute(tail, "lon", [(i, (i + 1) % count) for i in range(count)])
    right = lax.ppermute(head, "lon", [((i + 1) % count, i) for i in range(count)])
    gap = jnp.zeros(cells.shape[:2] + (width - 2 * RIM,), cells.dtype)
    return jnp.concatenate([right, gap, left], axis=2)


def tap_rows(kernel, row_count):
    taps = kernel.reshape(kernel.shape[0], KW, KW)
    return jnp.repeat(taps, row_count, axis=2)


def conv_channel(cells, rim, taps):
    row_count, width = cells.shape
    cells = cells.astype(jnp.float32)
    rim = rim.astype(jnp.float32)
    lane = lax.broadcasted_iota(jnp.int32, cells.shape, 1)
    shifted = []
    for b in range(KW):
        s = b - RIM
        if s == 0:
            moved = cells
        elif s > 0:
            moved = pltpu.roll(jnp.where(lane < s, rim, cells), width - s, 1)
        else:
            moved = pltpu.roll(jnp.where(lane >= width + s, rim, cells), -s, 1)
        shifted.append(moved.astype(jnp.bfloat16))
    shape = (row_count, KW * row_count)
    offset = (
        lax.rem(lax.broadcasted_iota(jnp.int32, shape, 1), row_count)
        - lax.broadcasted_iota(jnp.int32, shape, 0)
        + RIM
    )
    band = jnp.zeros(shape, jnp.float32)
    for a in range(KW):
        band = jnp.where(offset == a, taps[a : a + 1, :], band)
    return jnp.dot(
        band.astype(jnp.bfloat16),
        jnp.concatenate(shifted, axis=0),
        preferred_element_type=jnp.float32,
    )


def greet_peers(peers):
    me = lax.axis_index("ch")
    barrier = pltpu.get_barrier_semaphore()
    for r in range(1, peers):
        pl.semaphore_signal(
            barrier,
            inc=1,
            device_id={"ch": lax.rem(me + r, peers)},
            device_id_type=pl.DeviceIdType.MESH,
        )
    pl.semaphore_wait(barrier, peers - 1)


def forward_kernel(
    block,
    peers,
    state,
    rim,
    cot,
    mask,
    taps,
    bias,
    scale,
    conv_cells,
    grad_cells,
    conv_out,
    grad_branch,
    send_sem,
    recv_sem,
    own_sem,
):
    step = pl.program_id(0)
    steps = pl.num_programs(0)
    first = step * block
    me = lax.axis_index("ch")
    local_chan, row_count, _ = conv_out.shape
    quarter = row_count // peers
    pairs = ((conv_out, conv_cells), (grad_branch, grad_cells))

    def views(which, at, target):
        source, sink = pairs[which]
        rows = pl.ds(pl.multiple_of(target * quarter, quarter), quarter)
        return (
            source.at[pl.ds(at * block, block), rows, :],
            sink.at[pl.ds(me * local_chan + at * block, block)],
        )

    def remote(which, at, r):
        target = lax.rem(me + r, peers)
        source, sink = views(which, at, target)
        return pltpu.make_async_remote_copy(
            src_ref=source,
            dst_ref=sink,
            send_sem=send_sem.at[which, at, r - 1],
            recv_sem=recv_sem.at[which, at, r - 1],
            device_id={"ch": target},
            device_id_type=pl.DeviceIdType.MESH,
        )

    def own(which, at):
        source, sink = views(which, at, me)
        return pltpu.make_async_copy(source, sink, own_sem.at[which, at])

    @pl.when(step == 0)
    def _():
        greet_peers(peers)

    mask_f = mask[...].astype(jnp.float32)

    def channel(k, carry):
        conv = conv_channel(state[k], rim[k], taps[k])
        conv_out[first + k] = (conv + bias[first + k]).astype(jnp.bfloat16)
        grad_out = cot[k].astype(jnp.float32) * mask_f
        grad_branch[first + k] = (grad_out * scale[first + k]).astype(jnp.bfloat16)
        return carry

    lax.fori_loop(0, block, channel, 0, unroll=2)
    for which in range(2):
        for r in range(1, peers):
            remote(which, step, r).start()
        own(which, step).start()

    @pl.when(step == steps - 1)
    def _():
        def finish(at, carry):
            for which in range(2):
                for r in range(1, peers):
                    remote(which, at, r).wait()
                own(which, at).wait()
            return carry

        lax.fori_loop(0, steps, finish, 0)


def backward_kernel(
    block, state, branch, grad_conv, rim, cot, mask, taps, scale, updated, grad_state
):
    first = pl.program_id(0) * block
    mask_f = mask[...].astype(jnp.float32)

    def channel(k, carry):
        conv = conv_channel(grad_conv[k], rim[k], taps[k])
        grad_out = cot[k].astype(jnp.float32) * mask_f
        grad_state[k] = (grad_out + conv).astype(jnp.bfloat16)
        value = state[k].astype(jnp.float32) + scale[first + k] * branch[k].astype(jnp.float32)
        updated[k] = (mask_f * value).astype(jnp.bfloat16)
        return carry

    lax.fori_loop(0, block, channel, 0, unroll=2)


def math_kernel(
    hid_block,
    peers,
    conv_cells,
    grad_cells,
    gain,
    shift,
    win,
    win_t,
    bias_in,
    wout,
    wout_t,
    bias_out,
    branch,
    grad_conv,
    in_total,
    out_total,
    act,
    grad_pre,
    part_in,
    part_out,
    spread,
    outgoing,
    send_sem,
    recv_sem,
    own_sem,
):
    step = pl.program_id(0)
    steps = pl.num_programs(0)
    me = lax.axis_index("ch")
    full_width, block = conv_cells.shape
    hid = win.shape[1]
    local_chan = full_width // peers
    padded = branch.shape[0]
    sinks = (branch, grad_conv)

    def views(which, at, target):
        start = pl.multiple_of(me * (steps * block) + at * block, 128)
        return (
            outgoing.at[which, at, pl.ds(pl.multiple_of(target * padded, 16), padded), :],
            sinks[which].at[:, pl.ds(start, block)],
        )

    def remote(which, at, r):
        target = lax.rem(me + r, peers)
        source, sink = views(which, at, target)
        return pltpu.make_async_remote_copy(
            src_ref=source,
            dst_ref=sink,
            send_sem=send_sem.at[which, at, r - 1],
            recv_sem=recv_sem.at[which, at, r - 1],
            device_id={"ch": target},
            device_id_type=pl.DeviceIdType.MESH,
        )

    def own(which, at):
        source, sink = views(which, at, me)
        return pltpu.make_async_copy(source, sink, own_sem.at[which, at])

    def send(which, cells):
        for g in range(peers):
            spread[g * padded : g * padded + local_chan, :] = cells[
                g * local_chan : (g + 1) * local_chan, :
            ]
        outgoing[which, step] = spread[...].astype(jnp.bfloat16)
        for r in range(1, peers):
            remote(which, step, r).start()
        own(which, step).start()

    @pl.when(step == 0)
    def _():
        greet_peers(peers)
        part_in[...] = jnp.zeros_like(part_in)
        part_out[...] = jnp.zeros_like(part_out)
        spread[...] = jnp.zeros_like(spread)

    values = conv_cells[...].astype(jnp.float32)
    mean_val = jnp.sum(values, axis=0, keepdims=True) / full_width
    square = jnp.sum(values * values, axis=0, keepdims=True) / full_width
    inv_std = lax.rsqrt(square - mean_val * mean_val + norm_eps)
    centred = (values - mean_val) * inv_std
    normed = (centred * gain[...] + shift[...]).astype(jnp.bfloat16)
    grads = grad_cells[...]
    across = (((1,), (1,)), ((), ()))
    for start in range(0, hid, hid_block):
        here = slice(start, min(start + hid_block, hid))
        v = jnp.dot(win_t[here, :], normed, preferred_element_type=jnp.float32) + bias_in[here, :]
        tangent = jnp.tanh(root_coef * (v + cubic_coef * v * v * v))
        act_h = (0.5 * v * (1.0 + tangent)).astype(jnp.bfloat16)
        slope = 0.5 * (1.0 + tangent) + 0.5 * v * (1.0 - tangent * tangent) * root_coef * (
            1.0 + 3.0 * cubic_coef * v * v
        )
        grad_act = jnp.dot(wout[here, :], grads, preferred_element_type=jnp.float32)
        grad_h = (grad_act * slope).astype(jnp.bfloat16)
        act[here, :] = act_h
        grad_pre[here, :] = grad_h
        part_out[here, :] += lax.dot_general(
            act_h, grads, across, preferred_element_type=jnp.float32
        )
        part_in[here, :] += lax.dot_general(
            grad_h, normed, across, preferred_element_type=jnp.float32
        )
    grad_normed = jnp.dot(win[...], grad_pre[...], preferred_element_type=jnp.float32)
    scaled_grad = grad_normed * gain[...]
    mean_first = jnp.sum(scaled_grad, axis=0, keepdims=True) / full_width
    mean_second = jnp.sum(scaled_grad * centred, axis=0, keepdims=True) / full_width
    send(1, inv_std * (scaled_grad - mean_first - centred * mean_second))
    send(0, jnp.dot(wout_t[...], act[...], preferred_element_type=jnp.float32) + bias_out[...])

    @pl.when(step == steps - 1)
    def _():
        in_total[...] = part_in[...].astype(jnp.bfloat16)
        out_total[...] = part_out[...].astype(jnp.bfloat16)

        def finish(at, carry):
            for which in range(2):
                for r in range(1, peers):
                    remote(which, at, r).wait()
                own(which, at).wait()
            return carry

        lax.fori_loop(0, steps, finish, 0)


def block_math(conv_cells, grad_cells, gain, shift, win, bias_in, wout, bias_out):
    full_width, cells = conv_cells.shape
    hid = win.shape[1]
    peers = lax.axis_size("ch")
    padded = -(-(full_width // peers) // 16) * 16
    block = largest_divisor(cells // 128, 2) * 128
    steps = cells // block
    hid_block = 16 * largest_divisor(hid // 16, 20)
    tile = pl.BlockSpec((full_width, block), lambda i: (0, i))
    whole = lambda shape: pl.BlockSpec(shape, lambda i: (0, 0))
    anywhere = pl.BlockSpec(memory_space=pl.ANY)
    bf16 = jnp.bfloat16
    part = jax.ShapeDtypeStruct((hid, full_width), bf16)
    back = jax.ShapeDtypeStruct((padded, peers * cells), bf16)
    return pl.pallas_call(
        functools.partial(math_kernel, hid_block, peers),
        grid=(steps,),
        in_specs=[
            tile,
            tile,
            whole((full_width, 1)),
            whole((full_width, 1)),
            whole((full_width, hid)),
            whole((hid, full_width)),
            whole((hid, 1)),
            whole((hid, full_width)),
            whole((full_width, hid)),
            whole((full_width, 1)),
        ],
        out_specs=[anywhere, anywhere, whole((hid, full_width)), whole((hid, full_width))],
        out_shape=[back, back, part, part],
        scratch_shapes=[
            pltpu.VMEM((hid, block), bf16),
            pltpu.VMEM((hid, block), bf16),
            pltpu.VMEM((hid, full_width), jnp.float32),
            pltpu.VMEM((hid, full_width), jnp.float32),
            pltpu.VMEM((peers * padded, block), jnp.float32),
            pltpu.VMEM((2, steps, peers * padded, block), bf16),
            pltpu.SemaphoreType.DMA((2, steps, peers - 1)),
            pltpu.SemaphoreType.DMA((2, steps, peers - 1)),
            pltpu.SemaphoreType.DMA((2, steps)),
        ],
        compiler_params=pltpu.CompilerParams(
            vmem_limit_bytes=VMEM_LIMIT, collective_id=1, has_side_effects=True
        ),
        name="block_math",
    )(
        conv_cells,
        grad_cells,
        gain[:, None],
        shift[:, None],
        win,
        win.T,
        bias_in[:, None],
        wout,
        wout.T,
        bias_out[:, None],
    )


def body(
    ocean_state,
    sea_mask,
    kernel,
    conv_bias,
    norm_gain,
    norm_bias,
    weight_in,
    bias_in,
    weight_out,
    bias_out,
    layer_scale,
    cotangent,
):
    local_chan, row_count, lon_cells = ocean_state.shape
    chan_groups = lax.axis_size("ch")
    full_width = local_chan * chan_groups
    grad_scale = 1.0 / math.sqrt(row_count * lon_cells * lax.axis_size("lon"))
    block = largest_divisor(local_chan, 10)
    maps = pl.BlockSpec((block, row_count, lon_cells), lambda i: (i, 0, 0))
    one = pl.BlockSpec((row_count, lon_cells), lambda i: (0, 0))
    rows = pl.BlockSpec((block, KW, KW * row_count), lambda i: (i, 0, 0))
    scalars = pl.BlockSpec(memory_space=pltpu.SMEM)
    like = jax.ShapeDtypeStruct(ocean_state.shape, jnp.bfloat16)
    params = pltpu.CompilerParams(vmem_limit_bytes=VMEM_LIMIT)

    quarter = row_count // chan_groups
    steps = local_chan // block
    shares = jax.ShapeDtypeStruct((full_width, quarter, lon_cells), jnp.bfloat16)
    anywhere = pl.BlockSpec(memory_space=pl.ANY)
    conv_cells, grad_cells = pl.pallas_call(
        functools.partial(forward_kernel, block, chan_groups),
        grid=(steps,),
        in_specs=[maps, maps, maps, one, rows, scalars, scalars],
        out_specs=[anywhere, anywhere],
        out_shape=[shares, shares],
        scratch_shapes=[
            pltpu.VMEM(ocean_state.shape, jnp.bfloat16),
            pltpu.VMEM(ocean_state.shape, jnp.bfloat16),
            pltpu.SemaphoreType.DMA((2, steps, chan_groups - 1)),
            pltpu.SemaphoreType.DMA((2, steps, chan_groups - 1)),
            pltpu.SemaphoreType.DMA((2, steps)),
        ],
        compiler_params=pltpu.CompilerParams(
            vmem_limit_bytes=VMEM_LIMIT, collective_id=0, has_side_effects=True
        ),
        name="forward_conv",
    )(
        ocean_state,
        rim_exchange(ocean_state),
        cotangent,
        sea_mask,
        tap_rows(kernel, row_count),
        conv_bias,
        layer_scale,
    )
    branch, grad_conv, part_in, part_out = block_math(
        conv_cells.reshape(full_width, quarter * lon_cells),
        grad_cells.reshape(full_width, quarter * lon_cells),
        norm_gain,
        norm_bias,
        weight_in,
        bias_in,
        weight_out,
        bias_out,
    )
    sum_in, sum_out = lax.psum((part_in, part_out), ("lon", "ch"))
    branch, grad_conv = (
        cells[:local_chan].reshape(ocean_state.shape) for cells in (branch, grad_conv)
    )
    updated, grad_state = pl.pallas_call(
        functools.partial(backward_kernel, block),
        grid=(local_chan // block,),
        in_specs=[maps, maps, maps, maps, maps, one, rows, scalars],
        out_specs=[maps, maps],
        out_shape=[like, like],
        compiler_params=params,
        cost_estimate=pl.CostEstimate(flops=0, bytes_accessed=1, transcendentals=0),
        name="backward_conv",
    )(
        ocean_state,
        branch,
        grad_conv,
        rim_exchange(grad_conv),
        cotangent,
        sea_mask,
        tap_rows(kernel[:, ::-1], row_count),
        layer_scale,
    )
    return (
        updated,
        grad_state,
        sum_in.T.astype(jnp.float32) * grad_scale,
        sum_out.astype(jnp.float32) * grad_scale,
    )


def solution(mesh):
    return jax.shard_map(
        body,
        mesh=mesh,
        in_specs=(
            P("ch", None, "lon"),
            P(None, "lon"),
            P("ch", None),
            P("ch"),
            P(),
            P(),
            P(),
            P(),
            P(),
            P(),
            P("ch"),
            P("ch", None, "lon"),
        ),
        out_specs=(P("ch", None, "lon"), P("ch", None, "lon"), P(), P()),
        check_vma=False,
    )
```
